256 devices in a mesh: blk: 16 (over y, x_hi, core), grp: 16 (over x_lo, z).
Axes of the slice: x: 4 (x_hi: 2, x_lo: 2; x = x_hi * 2 + x_lo), y: 4, z: 8, core: 2. Of those that a mesh axis runs over, the one named last changes fastest.
Arguments:
- points: bfloat16 [32768, 1536], P(('blk', 'grp')), may hold values from -6 to 6
- centroids: bfloat16 [16384, 1536], P(('blk', 'grp')), may hold values from -0.15625 to 0.15625
- pair_blocks: int32 [16, 2], P('blk'), may hold values from 0 to 15, as said below
- pair_valid: int32 [16, 2], P('blk'), may hold values from 0 to 1, as said below
- sizes: int32 [16384], replicated, may hold values from 64 to 1024
Outputs:
- new_centroids: float32 [16384, 1536], P(('blk', 'grp'))
The draws below stay inside these ranges and needn't reach their ends.
Inputs may be any that keep to these rules, and one draw needn't show every extreme that they name: `pair_blocks`: column 0 is a permutation of the 16 centroid blocks; column 1 differs from column 0 in every row. `pair_valid`: column 0 is 1 in every row; column 1 is 0 in some rows.
All inputs are finite; a program needn't handle non-finite values.
Results may differ from the reference program's by a relative error of at most 0.0035.
Values may be sent and summed in bfloat16 or wider, within the bound.
No kernel may reach another device: no remote copies, remote signals or barrier semaphores. Data moves between devices by JAX's collectives and lax.ppermute only.
A program may use at most 128 MiB of HBM per device.

```python
import jax
import jax.numpy as jnp
from jax import lax

D = 1536
CB = 1024
ITERS = 4
NB = 16
PB = 2048
PTS = 32768
NC = 16384


def draw_pair_blocks(key, part):
    key = jax.random.fold_in(key, 11)
    first_key, second_key = jax.random.split(key)
    first = jax.random.permutation(first_key, NB).astype(jnp.int32)
    offset = jax.random.randint(second_key, (NB,), 1, NB).astype(jnp.int32)
    second = (first + offset) % NB
    return jnp.stack([first, second], axis=1).astype(jnp.int32)


def draw_pair_valid(key, part):
    key = jax.random.fold_in(key, 23)
    flag_key, spot_key = jax.random.split(key)
    second = jax.random.randint(flag_key, (NB,), 0, 2).astype(jnp.int32)
    spot = jax.random.randint(spot_key, (), 0, NB)
    second = second.at[spot].set(0)
    return jnp.stack([jnp.ones((NB,), jnp.int32), second], axis=1).astype(jnp.int32)


def set_ends(entries, key, smallest, top_value):
    longest = entries.shape.index(max(entries.shape))
    spots = []
    for shift in (0, 1):
        where = [jax.random.randint(jax.random.fold_in(key, axis), (), 0, length) for axis, length in enumerate(entries.shape)]
        where[longest] = (where[longest] + shift) % entries.shape[longest]
        spots.append(tuple(where))
    return entries.at[spots[0]].set(smallest).at[spots[1]].set(top_value)


def level_of(rng, shape, cuts, least, top_value):
    level, own = 1.0, jax.random.fold_in(rng, 6)
    for position, parts in cuts:
        steps = jnp.exp(jax.random.uniform(jax.random.fold_in(own, position), (parts,), jnp.float32, least / len(cuts), top_value / len(cuts)))
        level = level * jnp.repeat(steps, shape[position] // parts).reshape([-1 if axis == position else 1 for axis in range(len(shape))])
    return level


def gaussian(rng, extent, deviation, limit, shards=(), kind=jnp.bfloat16):
    result = jax.random.normal(rng, extent, jnp.float32) * deviation
    if len(shards) > 0:
        result = level_of(rng, extent, shards, -0.22, 0.18) * result
    return jnp.clip(result, min=-limit, max=limit).astype(kind)


def setup_inputs(seed: int = 0) -> dict:
    key_list = jax.random.split(jax.random.key(seed), 6)
    return {
        "points": gaussian(key_list[0], (PTS, D), 1.0, 6.0, ((0, 256),)),
        "centroids": gaussian(key_list[1], (NC, D), D ** -0.5, 0.15625, ((0, 256),)),
        "pair_blocks": draw_pair_blocks(jax.random.fold_in(key_list[5], 71), 0),
        "pair_valid": draw_pair_valid(jax.random.fold_in(key_list[5], 71), 0),
        "sizes": set_ends(jax.random.randint(key_list[4], (NC,), 64, 1025), jax.random.fold_in(key_list[4], 1), 64, 1024).astype(jnp.int32),
    }


SCALE = 3.0


def pair_kernel(block_points, pair_cents, valid):
    dots = jnp.einsum("rd,knd->rkn", block_points.astype(jnp.float32), pair_cents.astype(jnp.float32), precision=lax.Precision.HIGHEST)
    return jnp.exp(SCALE * dots) * valid[None, :, None]


def reference(points, centroids, pair_blocks, pair_valid, sizes):
    blocks_x = points.reshape(NB, PB, D)
    cents = centroids.reshape(NB, CB, D)
    valid = pair_valid.astype(jnp.float32)
    size_f = sizes.astype(jnp.float32)
    targets = (size_f * (jnp.float32(PTS) / jnp.sum(size_f))).reshape(NB, CB)
    choose = (pair_blocks[:, :, None] == jnp.arange(NB, dtype=jnp.int32)[None, None, :]).astype(jnp.float32) * valid[:, :, None]
    scale_v = jnp.ones((NB, CB), jnp.float32)
    scale_u = jnp.zeros((NB, PB), jnp.float32)
    for step in range(ITERS):
        def sweep(item, scale_v=scale_v):
            block_points, pair, okay = item
            kernel = pair_kernel(block_points, cents[pair], okay)
            rowsum = jnp.einsum("rkc,kc->r", kernel, scale_v[pair], precision=lax.Precision.HIGHEST)
            inverse = 1.0 / rowsum
            colpart = jnp.einsum("rkc,r->kc", kernel, inverse, precision=lax.Precision.HIGHEST)
            return inverse, colpart
        scale_u, colparts = lax.map(sweep, (blocks_x, pair_blocks, valid))
        totals = jnp.einsum("pkb,pkc->bc", choose, colparts, precision=lax.Precision.HIGHEST)
        scale_v = targets / totals

    def accumulate(total, item):
        block_points, pair, okay, inverse, hot = item
        kernel = pair_kernel(block_points, cents[pair], okay)
        weights = (inverse[:, None, None] * kernel * scale_v[pair][None]).astype(jnp.bfloat16)
        part = jnp.einsum("rkc,rd->kcd", weights.astype(jnp.float32), block_points.astype(jnp.float32), precision=lax.Precision.HIGHEST)
        return total + jnp.einsum("kb,kcd->bcd", hot, part, precision=lax.Precision.HIGHEST), None

    sums, unused = lax.scan(accumulate, jnp.zeros((NB, CB, D), jnp.float32), (blocks_x, pair_blocks, valid, scale_u, choose))
    return (sums / targets[:, :, None]).reshape(NC, D)
```

```python
import jax
import jax.numpy as jnp
from jax import lax
from jax.sharding import Mesh, PartitionSpec as P

ITERS = 4
SCALE = 3.0
NY, NXH, NC, NXL, NZ = 4, 2, 2, 2, 8
NB = NY * NXH * NC
PLANE = ("y", "xh", "c", "xl")
SWAP = [(0, 1), (1, 0)]


def ordered(first, mine, other):
    is0 = first == 0
    return jnp.stack([jnp.where(is0, mine, other), jnp.where(is0, other, mine)])


def exchange(row, axes, n):
    return lax.all_to_all(jnp.broadcast_to(row[None], (n,) + row.shape), axes, 0, 0)


def shards(points, centroids, pair_blocks, pair_valid, sizes):
    width = points.shape[1]
    c = lax.axis_index("c")
    xl = lax.axis_index("xl")
    z = lax.axis_index("z")
    slots = pair_blocks[0]
    valid = pair_valid[0].astype(jnp.float32)

    pts = lax.all_gather(points, "z", axis=0, tiled=True)

    slots_other = lax.ppermute(slots, "c", SWAP)
    halves = centroids.reshape(2, 32, width)
    mine = lax.dynamic_index_in_dim(halves, c, 0, keepdims=False)
    give = lax.dynamic_index_in_dim(halves, 1 - c, 0, keepdims=False)
    got = lax.ppermute(give, "c", SWAP)
    both = ordered(c, mine, got)
    allc = lax.all_to_all(
        jnp.broadcast_to(both[None], (NY * NXH,) + both.shape), ("y", "xh"), 0, 0
    ).reshape(NB, 32, width)
    sel_mine = jnp.take(allc, slots, axis=0)
    sel_give = jnp.take(allc, slots_other, axis=0)
    sel_got = lax.ppermute(sel_give, "c", SWAP)
    kept = jnp.swapaxes(ordered(c, sel_mine, sel_got), 0, 1).reshape(2, 64, width)
    kept_xl = lax.ppermute(kept, "xl", SWAP)
    cents = jnp.swapaxes(ordered(xl, kept, kept_xl), 0, 1).reshape(256, width)

    size_f = sizes.astype(jnp.float32)
    targets = size_f * (jnp.float32(points.shape[0] * 256) / jnp.sum(size_f))
    table = jnp.take(targets.reshape(NB, 2, NZ, 64), z, axis=2).reshape(NB, 128)
    target_pair = jnp.take(table, slots, axis=0)

    dots = lax.dot_general(
        cents, pts, (((1,), (1,)), ((), ())), preferred_element_type=jnp.float32
    )
    kt = (jnp.exp(SCALE * dots).reshape(2, 128, -1) * valid[:, None, None]).reshape(256, -1)

    ids = jnp.pad(slots.astype(jnp.float32), (0, 126))

    def totals_of(colpart):
        got = exchange(jnp.concatenate([colpart, ids]), PLANE, NB * NXL)
        got_ids = got[:, 256:258].astype(jnp.int32)
        match = (got_ids[None] == slots[:, None, None]).astype(jnp.float32)
        cols = got[:, :256].reshape(-1, 2, 128)
        return jnp.sum(match[..., None] * cols[None], axis=(1, 2))

    scale_v = jnp.ones((256,), jnp.float32)
    for step in range(ITERS):
        rowpart = jnp.sum(kt * scale_v[:, None], axis=0)
        scale_u = 1.0 / jnp.sum(exchange(rowpart, "z", NZ), axis=0)
        if step < ITERS - 1:
            colpart = jnp.sum(kt * scale_u[None, :], axis=1)
            scale_v = (target_pair / totals_of(colpart)).reshape(256)
    weights = scale_u[None, :] * kt * scale_v[:, None]
    tot = totals_of(jnp.sum(weights, axis=1))
    sums = lax.dot_general(
        weights.astype(jnp.bfloat16), pts, (((1,), (0,)), ((), ())), preferred_element_type=jnp.float32
    ).reshape(2, 2, 64, width)
    s_mine = lax.dynamic_index_in_dim(sums, xl, 1, keepdims=False)
    s_give = lax.dynamic_index_in_dim(sums, 1 - xl, 1, keepdims=False).astype(jnp.bfloat16)
    s_got = lax.ppermute(s_give, "xl", SWAP)
    tot_mine = lax.dynamic_index_in_dim(tot.reshape(2, 2, 64), xl, 1, keepdims=False)
    means = ((s_mine + s_got.astype(jnp.float32)) / tot_mine[:, :, None]).astype(jnp.bfloat16)
    means = means.reshape(2, 2, 32, width)
    m_mine = lax.dynamic_index_in_dim(means, c, 1, keepdims=False)
    m_give = lax.dynamic_index_in_dim(means, 1 - c, 1, keepdims=False)
    m_got = lax.ppermute(m_give, "c", SWAP)

    blocks = jnp.arange(NB, dtype=jnp.int32)
    spread = jnp.zeros((NB, 32, width), jnp.float32)
    for part, ids_of, k in ((m_mine, slots, 0), (m_mine, slots, 1), (m_got, slots_other, 0), (m_got, slots_other, 1)):
        hit = (blocks == ids_of[k])[:, None, None]
        spread = spread + jnp.where(hit, part[k][None].astype(jnp.float32), 0.0)
    spread = spread.astype(jnp.bfloat16).reshape(NY * NXH, 2, 32, width)
    landed = lax.all_to_all(spread, ("y", "xh"), 0, 0)
    owned = jnp.sum(landed.astype(jnp.float32), axis=0)
    o_mine = lax.dynamic_index_in_dim(owned, c, 0, keepdims=False)
    o_give = lax.dynamic_index_in_dim(owned, 1 - c, 0, keepdims=False)
    o_got = lax.ppermute(o_give, "c", SWAP)
    return ordered(c, o_mine, o_got).reshape(64, width)


def solution(mesh):
    fine = Mesh(mesh.devices.reshape(NY, NXH, NC, NXL, NZ), ("y", "xh", "c", "xl", "z"))
    rows = P(("y", "xh", "c", "xl", "z"), None)
    pair = P(("y", "xh", "c"), None)
    return jax.shard_map(
        shards, mesh=fine, in_specs=(rows, rows, pair, pair, P()), out_specs=rows, check_vma=False
    )
```

```python
import jax
import jax.numpy as jnp
from jax import lax
from jax.sharding import Mesh, PartitionSpec as P

ITERS = 4
SCALE = 3.0
NY, NXH, NC, NXL, NZ = 4, 2, 2, 2, 8
NB = NY * NXH * NC
PLANE = ("y", "xh", "c", "xl")
SWAP = [(0, 1), (1, 0)]
UP = [(i, (i + 1) % NZ) for i in range(NZ)]
DOWN = [(i, (i - 1) % NZ) for i in range(NZ)]
after = lax.optimization_barrier


def ordered(first, mine, other):
    is0 = first == 0
    return jnp.stack([jnp.where(is0, mine, other), jnp.where(is0, other, mine)])


def exchange(row, axes, n):
    return lax.all_to_all(jnp.broadcast_to(row[None], (n,) + row.shape), axes, 0, 0)


def shards(points, centroids, pair_blocks, pair_valid, sizes):
    rows, width = points.shape
    c = lax.axis_index("c")
    xl = lax.axis_index("xl")
    z = lax.axis_index("z")
    me = lax.axis_index(("y", "xh", "c"))
    def put(buf, part, at):
        return lax.dynamic_update_slice(buf, part[None], (at % NZ, 0, 0))

    spread_cents = jnp.broadcast_to(centroids[None], (NY * NXH,) + centroids.shape)
    allc = lax.all_to_all(spread_cents, ("y", "xh"), 0, 0)
    up1 = lax.ppermute(points, "z", UP)
    down1 = lax.ppermute(points, "z", DOWN)
    pair_blocks, points, sizes, pair_valid, _ = after((pair_blocks, points, sizes, pair_valid, up1))
    slots = pair_blocks[0]
    valid = pair_valid[0].astype(jnp.float32)
    slots_other = lax.ppermute(slots, "c", SWAP)
    ids4 = jnp.concatenate([slots, slots_other])
    grid = lax.broadcasted_iota(jnp.int32, (4, NY * NXH, NC), 1) * NC + lax.broadcasted_iota(
        jnp.int32, (4, NY * NXH, NC), 2
    )
    hits = ids4[:, None, None] == grid
    up2 = lax.ppermute(up1, "z", UP)
    down2 = lax.ppermute(down1, "z", DOWN)
    pts = put(jnp.zeros((NZ, rows, width), points.dtype), points, z)
    pts = put(put(pts, up1, z - 1 + NZ), down1, z + 1)
    up3 = lax.ppermute(up2, "z", UP)
    down3 = lax.ppermute(down2, "z", DOWN)
    pts = put(put(pts, up2, z - 2 + NZ), down2, z + 2)

    allc, _ = after((allc, up2))
    sel_give = allc.at[slots_other // NC].get(mode="promise_in_bounds")
    sel_got = lax.ppermute(sel_give, "c", SWAP)
    sel_mine = allc.at[slots // NC].get(mode="promise_in_bounds")
    kept = jnp.where((slots % NC == c)[:, None, None], sel_mine, sel_got)
    kept_xl = lax.ppermute(kept, "xl", SWAP)
    far = lax.ppermute(up3, "z", UP)
    pts = put(put(pts, up3, z - 3 + NZ), down3, z + 3)
    pts = put(pts, far, z + 4).reshape(NZ * rows, width)
    cents = jnp.swapaxes(ordered(xl, kept, kept_xl), 0, 1).reshape(256, width)

    size_f = sizes.astype(jnp.float32)
    targets = size_f * (jnp.float32(points.shape[0] * 256) / jnp.sum(size_f))
    table = lax.dynamic_index_in_dim(targets.reshape(NB, 2, NZ, 64), z, 2, keepdims=False).reshape(NB, 128)
    target_pair = table.at[slots].get(mode="promise_in_bounds")

    dots = lax.dot_general(
        cents, pts, (((1,), (1,)), ((), ())), preferred_element_type=jnp.float32
    )
    kt = (jnp.exp(SCALE * dots).reshape(2, 128, -1) * valid[:, None, None]).reshape(256, -1)

    ids = jnp.pad(slots.astype(jnp.float32), (0, 126))
    kt, target_pair, ids, hits, slots, me = after((kt, target_pair, ids, hits, slots, me))

    def totals_of(match, got):
        return jnp.sum(match[..., None] * got[:, :256].reshape(1, -1, 2, 128), axis=(1, 2))

    scale_v = jnp.ones((256,), jnp.float32)
    for step in range(ITERS):
        rowpart = jnp.sum(kt * scale_v[:, None], axis=0)
        scale_u = 1.0 / jnp.sum(exchange(rowpart, "z", NZ), axis=0)
        if step < ITERS - 1:
            colpart = jnp.sum(kt * scale_u[None, :], axis=1)
            if step == 0:
                got = exchange(jnp.concatenate([colpart, ids]), PLANE, NB * NXL)
                got_ids = got[:, 256:258].astype(jnp.int32)
                match = (got_ids[None] == slots[:, None, None]).astype(jnp.float32)
                match_me = (got_ids[None] == me).astype(jnp.float32)
                got, match, match_me = after((got, match, match_me))
            else:
                got = exchange(colpart, PLANE, NB * NXL)
            scale_v = (target_pair / totals_of(match, got)).reshape(256)
    weights = scale_u[None, :] * kt * scale_v[:, None]
    weights = weights.astype(jnp.bfloat16)
    colpart = jnp.sum(weights.astype(jnp.float32), axis=1)

    parts = []
    tot = exchange(colpart, PLANE, NB * NXL)
    for k in (0, 1):
        sums = lax.dot_general(
            weights[128 * k : 128 * (k + 1)], pts, (((1,), (0,)), ((), ())), preferred_element_type=jnp.float32
        ).reshape(2, 64, width)
        mine = lax.dynamic_index_in_dim(sums, xl, 0, keepdims=False)
        give = lax.dynamic_index_in_dim(sums, 1 - xl, 0, keepdims=False).astype(jnp.bfloat16)
        got = lax.ppermute(give, "xl", SWAP)
        sums = (mine + got.astype(jnp.float32)).astype(jnp.bfloat16).reshape(2, 32, width)
        m_mine = lax.dynamic_index_in_dim(sums, c, 0, keepdims=False)
        m_give = lax.dynamic_index_in_dim(sums, 1 - c, 0, keepdims=False)
        m_got = lax.ppermute(m_give, "c", SWAP)
        parts += [m_mine, m_got]
    zero = jnp.zeros((), jnp.bfloat16)

    def placed(first, second, a, b):
        return jnp.where(first[:, :, None, None], a, jnp.where(second[:, :, None, None], b, zero))

    parts, tot = after((parts, tot))
    spread = placed(hits[0], hits[1], parts[0], parts[2]) + placed(hits[2], hits[3], parts[1], parts[3])
    landed = lax.all_to_all(spread, ("y", "xh"), 0, 0)
    owned = jnp.sum(landed.astype(jnp.float32), axis=0)
    o_mine = lax.dynamic_index_in_dim(owned, c, 0, keepdims=False)
    o_give = lax.dynamic_index_in_dim(owned, 1 - c, 0, keepdims=False)
    o_got = lax.ppermute(o_give, "c", SWAP)
    tot = totals_of(match_me, tot).reshape(2, 64)
    tot = lax.dynamic_index_in_dim(tot, xl, 0, keepdims=False)
    return ordered(c, o_mine, o_got).reshape(64, width) / tot[:, None]


def solution(mesh):
    fine = Mesh(mesh.devices.reshape(NY, NXH, NC, NXL, NZ), ("y", "xh", "c", "xl", "z"))
    rows = P(("y", "xh", "c", "xl", "z"), None)
    pair = P(("y", "xh", "c"), None)
    return jax.shard_map(
        shards, mesh=fine, in_specs=(rows, rows, pair, pair, P()), out_specs=rows, check_vma=False
    )
```

```python
import jax
import jax.numpy as jnp
import numpy as np
from jax import lax
from jax.sharding import Mesh, PartitionSpec as P

ITERS = 4
SCALE = 3.0
NY, NXH, NC, NXL, NZ = 4, 2, 2, 2, 8
NB = NY * NXH * NC
PLANE = ("y", "xh", "c", "xl")
SWAP = [(0, 1), (1, 0)]
UP = [(i, (i + 1) % NZ) for i in range(NZ)]
DOWN = [(i, (i - 1) % NZ) for i in range(NZ)]
after = lax.optimization_barrier


def ordered(first, mine, other):
    is0 = first == 0
    return jnp.stack([jnp.where(is0, mine, other), jnp.where(is0, other, mine)])


def exchange(row, axes, n):
    return lax.all_to_all(jnp.broadcast_to(row[None], (n,) + row.shape), axes, 0, 0)


def shards(points, centroids, pair_blocks, pair_valid, sizes):
    rows, width = points.shape
    c = lax.axis_index("c")
    xl = lax.axis_index("xl")
    z = lax.axis_index("z")
    def put(buf, part, at):
        return lax.dynamic_update_slice(buf, part[None], (at % NZ, 0, 0))

    spread_cents = jnp.broadcast_to(centroids[None], (NY * NXH,) + centroids.shape)
    allc = lax.all_to_all(spread_cents, ("y", "xh"), 0, 0)
    up1 = lax.ppermute(points, "z", UP)
    down1 = lax.ppermute(points, "z", DOWN)
    pair_blocks, points, _ = after((pair_blocks, points, up1))
    slots = pair_blocks[0]
    slots_other = lax.ppermute(slots, "c", SWAP)
    up2 = lax.ppermute(up1, "z", UP)
    down2 = lax.ppermute(down1, "z", DOWN)
    pts = put(jnp.zeros((NZ, rows, width), points.dtype), points, z)
    pts = put(put(pts, up1, z - 1 + NZ), down1, z + 1)
    up3 = lax.ppermute(up2, "z", UP)
    down3 = lax.ppermute(down2, "z", DOWN)
    pts = put(put(pts, up2, z - 2 + NZ), down2, z + 2)

    allc, _ = after((allc, up2))
    sel_give = allc.at[slots_other // NC].get(mode="promise_in_bounds")
    sel_got = lax.ppermute(sel_give, "c", SWAP)
    sel_mine = allc.at[slots // NC].get(mode="promise_in_bounds")
    kept = jnp.where((slots % NC == c)[:, None, None], sel_mine, sel_got)
    kept_xl = lax.ppermute(kept, "xl", SWAP)
    far, _ = after((up3, kept))
    far = lax.ppermute(far, "z", UP)
    pts = put(put(pts, up3, z - 3 + NZ), down3, z + 3)
    cents = jnp.swapaxes(ordered(xl, kept, kept_xl), 0, 1).reshape(256, width)

    valid = pair_valid[0].astype(jnp.float32)

    def kernel_of(part):
        dots = lax.dot_general(
            cents, part, (((1,), (1,)), ((), ())), preferred_element_type=jnp.float32
        )
        return (jnp.exp(SCALE * dots).reshape(2, 128, -1) * valid[:, None, None]).reshape(256, -1)

    kt = kernel_of(pts.reshape(NZ * rows, width))
    kt = lax.dynamic_update_slice(kt, kernel_of(far), (0, ((z + 4) % NZ) * rows))
    pts = put(pts, far, z + 4).reshape(NZ * rows, width)

    def totals_of(match, got):
        return jnp.sum(match[..., None] * got[:, :256].reshape(1, -1, 2, 128), axis=(1, 2))

    rowpart = jnp.sum(kt, axis=0)
    rowpart, sizes, slots, slots_other = after((rowpart, sizes, slots, slots_other))
    got = exchange(rowpart, "z", NZ)
    ids = jnp.pad(slots.astype(jnp.float32), (0, 126))
    per_row = NB * 8
    pick = (8 * slots[:, None] + 4 * jnp.arange(2, dtype=jnp.int32)[None, :] + z // 2).reshape(4)
    own = sizes.reshape(per_row, 128).at[pick].get(mode="promise_in_bounds")
    own = lax.dynamic_slice(own, (0, (z % 2) * 64), (4, 64)).reshape(2, 128)
    factor = jnp.float32(rows * 256) / jnp.sum(sizes.astype(jnp.float32))
    target_pair = own.astype(jnp.float32) * factor
    grid = lax.broadcasted_iota(jnp.int32, (4, NY * NXH, NC), 1) * NC + lax.broadcasted_iota(
        jnp.int32, (4, NY * NXH, NC), 2
    )
    hits = jnp.concatenate([slots, slots_other])[:, None, None] == grid
    hits = [hits[i] for i in range(4)]
    got, ids, target_pair, hits, slots, pts = after((got, ids, target_pair, hits, slots, pts))

    for step in range(ITERS):
        if step > 0:
            got = exchange(jnp.sum(kt * scale_v[:, None], axis=0), "z", NZ)
        scale_u = 1.0 / jnp.sum(got, axis=0)
        if step < ITERS - 1:
            colpart = jnp.sum(kt * scale_u[None, :], axis=1)
            if step == 0:
                got = exchange(jnp.concatenate([colpart, ids]), PLANE, NB * NXL)
                got_ids = got[:, 256:258].astype(jnp.int32)
                match = (got_ids[None] == slots[:, None, None]).astype(jnp.float32)
                got, match = after((got, match))
            else:
                got = exchange(colpart, PLANE, NB * NXL)
            scale_v = (target_pair / totals_of(match, got)).reshape(256)
    weights = (scale_u[None, :] * kt * scale_v[:, None]).astype(jnp.bfloat16)

    def halved(part, at, axis_name):
        mine = lax.dynamic_index_in_dim(part, at, 0, keepdims=False)
        give = lax.dynamic_index_in_dim(part, 1 - at, 0, keepdims=False)
        return mine, lax.ppermute(give, axis_name, SWAP)

    ones = jnp.ones((NZ * rows, 128), jnp.bfloat16)
    tots = lax.dot_general(weights, ones, (((1,), (0,)), ((), ())), preferred_element_type=jnp.float32)
    tots = tots.reshape(2, 2, 64, 128)
    tots = jnp.swapaxes(tots, 0, 1)
    t_mine, t_got = halved(tots, xl, "xl")
    tots = jnp.swapaxes((t_mine + t_got).reshape(2, 2, 32, 128), 0, 1)
    tots = halved(tots, c, "c")

    def in_thirds(value, first):
        at = np.eye(128, dtype=np.float32)[first : first + 3]
        high = lax.reduce_precision(value, 8, 7)
        rest = value - high
        middle = lax.reduce_precision(rest, 8, 7)
        low = rest - middle
        return (high * at[:1] + middle * at[1:2] + low * at[2:]).astype(jnp.bfloat16)

    parts = []
    for k in (0, 1):
        sums = lax.dot_general(
            weights[128 * k : 128 * (k + 1)], pts, (((1,), (0,)), ((), ())), preferred_element_type=jnp.float32
        ).reshape(2, 64, width)
        mine = lax.dynamic_index_in_dim(sums, xl, 0, keepdims=False)
        give = lax.dynamic_index_in_dim(sums, 1 - xl, 0, keepdims=False).astype(jnp.bfloat16)
        got = lax.ppermute(give, "xl", SWAP)
        sums = (mine + got.astype(jnp.float32)).astype(jnp.bfloat16).reshape(2, 32, width)
        pair = halved(sums, c, "c")
        parts.append([jnp.concatenate([pair[i], in_thirds(tots[i][k], 4 * i)], axis=1) for i in (0, 1)])
    zero = jnp.zeros((), jnp.bfloat16)

    def placed(first, second, a, b):
        return jnp.where(first[:, :, None, None], a, jnp.where(second[:, :, None, None], b, zero))

    spread = placed(hits[0], hits[1], parts[0][0], parts[1][0]) + placed(hits[2], hits[3], parts[0][1], parts[1][1])
    landed = lax.all_to_all(spread, ("y", "xh"), 0, 0)
    owned = jnp.sum(landed.astype(jnp.float32), axis=0)
    owned = owned[:, :, :width] / jnp.sum(owned[:, :, width:], axis=2, keepdims=True)
    o_mine, o_got = halved(owned, c, "c")
    return ordered(c, o_mine, o_got).reshape(64, width)


def solution(mesh):
    fine = Mesh(mesh.devices.reshape(NY, NXH, NC, NXL, NZ), ("y", "xh", "c", "xl", "z"))
    rows = P(("y", "xh", "c", "xl", "z"), None)
    pair = P(("y", "xh", "c"), None)
    return jax.shard_map(
        shards, mesh=fine, in_specs=(rows, rows, pair, pair, P()), out_specs=rows, check_vma=False
    )
```

```python
import jax
import jax.numpy as jnp
import numpy as np
from jax import lax
from jax.sharding import Mesh, PartitionSpec as P

ITERS = 4
SCALE = 3.0
NY, NXH, NC, NXL, NZ = 4, 2, 2, 2, 8
NB = NY * NXH * NC
PLANE = ("y", "xh", "c", "xl")
SWAP = [(0, 1), (1, 0)]
UP = [(i, (i + 1) % NZ) for i in range(NZ)]
DOWN = [(i, (i - 1) % NZ) for i in range(NZ)]
after = lax.optimization_barrier


def ordered(first, mine, other):
    is0 = first == 0
    return jnp.stack([jnp.where(is0, mine, other), jnp.where(is0, other, mine)])


def exchange(row, axes, n):
    return lax.all_to_all(jnp.broadcast_to(row[None], (n,) + row.shape), axes, 0, 0)


def shards(points, centroids, pair_blocks, pair_valid, sizes):
    rows, width = points.shape
    c = lax.axis_index("c")
    xl = lax.axis_index("xl")
    z = lax.axis_index("z")
    def put(buf, part, at):
        return lax.dynamic_update_slice(buf, part[None], (at % NZ, 0, 0))

    spread_cents = jnp.broadcast_to(centroids[None], (NY * NXH,) + centroids.shape)
    allc = lax.all_to_all(spread_cents, ("y", "xh"), 0, 0)
    up1 = lax.ppermute(points, "z", UP)
    down1 = lax.ppermute(points, "z", DOWN)
    pair_blocks, points, _ = after((pair_blocks, points, up1))
    slots = pair_blocks[0]
    slots_other = lax.ppermute(slots, "c", SWAP)
    up2 = lax.ppermute(up1, "z", UP)
    down2 = lax.ppermute(down1, "z", DOWN)
    pts = jnp.broadcast_to(points[None], (NZ + 2, rows, width))
    pts = put(put(pts, up1, z - 1 + NZ), down1, z + 1)
    up3 = lax.ppermute(up2, "z", UP)
    down3 = lax.ppermute(down2, "z", DOWN)
    pts = put(put(pts, up2, z - 2 + NZ), down2, z + 2)

    allc, _ = after((allc, up2))
    sel_give = allc.at[slots_other // NC].get(mode="promise_in_bounds")
    sel_got = lax.ppermute(sel_give, "c", SWAP)
    sel_mine = allc.at[slots // NC].get(mode="promise_in_bounds")
    kept = jnp.where((slots % NC == c)[:, None, None], sel_mine, sel_got)
    kept_xl = lax.ppermute(kept, "xl", SWAP)
    up3, down3, _ = after((up3, down3, kept))
    far = lax.ppermute(up3, "z", UP)
    pts = put(put(pts, up3, z - 3 + NZ), down3, z + 3)
    cents = jnp.swapaxes(ordered(xl, kept, kept_xl), 0, 1).reshape(256, width)

    valid = pair_valid[0].astype(jnp.float32)

    def kernel_of(part):
        dots = lax.dot_general(
            cents, part, (((1,), (1,)), ((), ())), preferred_element_type=jnp.float32
        )
        return (jnp.exp(SCALE * dots).reshape(2, 128, -1) * valid[:, None, None]).reshape(256, -1)

    kt = kernel_of(pts[:NZ].reshape(NZ * rows, width))
    kt = lax.dynamic_update_slice(kt, kernel_of(far), (0, ((z + 4) % NZ) * rows))
    pts = put(pts, far, z + 4)

    def totals_of(match, got):
        return jnp.sum(match[..., None] * got[:, :256].reshape(1, -1, 2, 128), axis=(1, 2))

    rowpart = jnp.sum(kt, axis=0)
    rowpart, sizes, slots, slots_other = after((rowpart, sizes, slots, slots_other))
    got = exchange(rowpart, "z", NZ)
    ids = jnp.pad(slots.astype(jnp.float32), (0, 126))
    per_row = NB * 8
    pick = (8 * slots[:, None] + 4 * jnp.arange(2, dtype=jnp.int32)[None, :] + z // 2).reshape(4)
    own = sizes.reshape(per_row, 128).at[pick].get(mode="promise_in_bounds")
    own = lax.dynamic_slice(own, (0, (z % 2) * 64), (4, 64)).reshape(2, 128)
    factor = jnp.float32(rows * 256) / jnp.sum(sizes.astype(jnp.float32))
    target_pair = own.astype(jnp.float32) * factor
    grid = lax.broadcasted_iota(jnp.int32, (4, NY * NXH, NC), 1) * NC + lax.broadcasted_iota(
        jnp.int32, (4, NY * NXH, NC), 2
    )
    hits = jnp.concatenate([slots, slots_other])[:, None, None] == grid
    hits = [hits[i] for i in range(4)]
    got, ids, target_pair, hits, slots, pts = after((got, ids, target_pair, hits, slots, pts))
    pts = pts[:NZ].reshape(NZ * rows, width)

    for step in range(ITERS):
        if step > 0:
            got = exchange(jnp.sum(kt * scale_v[:, None], axis=0), "z", NZ)
        scale_u = 1.0 / jnp.sum(got, axis=0)
        if step < ITERS - 1:
            colpart = jnp.sum(kt * scale_u[None, :], axis=1)
            if step == 0:
                got = exchange(jnp.concatenate([colpart, ids]), PLANE, NB * NXL)
                got_ids = got[:, 256:258].astype(jnp.int32)
                match = (got_ids[None] == slots[:, None, None]).astype(jnp.float32)
                got, match = after((got, match))
            else:
                got = exchange(colpart, PLANE, NB * NXL)
            scale_v = (target_pair / totals_of(match, got)).reshape(256)
    weights = (scale_u[None, :] * kt * scale_v[:, None]).astype(jnp.bfloat16)

    def halved(part, at, axis_name):
        mine = lax.dynamic_index_in_dim(part, at, 0, keepdims=False)
        give = lax.dynamic_index_in_dim(part, 1 - at, 0, keepdims=False)
        return mine, lax.ppermute(give, axis_name, SWAP)

    ones = jnp.ones((NZ * rows, 128), jnp.bfloat16)
    tots = lax.dot_general(weights, ones, (((1,), (0,)), ((), ())), preferred_element_type=jnp.float32)
    tots = tots.reshape(2, 2, 64, 128)
    tots = jnp.swapaxes(tots, 0, 1)
    t_mine, t_got = halved(tots, xl, "xl")
    tots = jnp.swapaxes((t_mine + t_got).reshape(2, 2, 32, 128), 0, 1)
    tots = halved(tots, c, "c")

    def in_thirds(value, first):
        at = np.eye(128, dtype=np.float32)[first : first + 3]
        high = lax.reduce_precision(value, 8, 7)
        rest = value - high
        middle = lax.reduce_precision(rest, 8, 7)
        low = rest - middle
        return (high * at[:1] + middle * at[1:2] + low * at[2:]).astype(jnp.bfloat16)

    parts = []
    for k in (0, 1):
        sums = lax.dot_general(
            weights[128 * k : 128 * (k + 1)], pts, (((1,), (0,)), ((), ())), preferred_element_type=jnp.float32
        ).reshape(2, 64, width)
        mine = lax.dynamic_index_in_dim(sums, xl, 0, keepdims=False)
        give = lax.dynamic_index_in_dim(sums, 1 - xl, 0, keepdims=False).astype(jnp.bfloat16)
        got = lax.ppermute(give, "xl", SWAP)
        sums = (mine + got.astype(jnp.float32)).astype(jnp.bfloat16).reshape(2, 32, width)
        pair = halved(sums, c, "c")
        parts.append([jnp.concatenate([pair[i], in_thirds(tots[i][k], 4 * i)], axis=1) for i in (0, 1)])
    zero = jnp.zeros((), jnp.bfloat16)

    def placed(first, second, a, b):
        return jnp.where(first[:, :, None, None], a, jnp.where(second[:, :, None, None], b, zero))

    spread = placed(hits[0], hits[1], parts[0][0], parts[1][0]) + placed(hits[2], hits[3], parts[0][1], parts[1][1])
    landed = lax.all_to_all(spread, ("y", "xh"), 0, 0)
    owned = jnp.sum(landed.astype(jnp.float32), axis=0)
    owned = owned[:, :, :width] / jnp.sum(owned[:, :, width:], axis=2, keepdims=True)
    o_mine, o_got = halved(owned, c, "c")
    return ordered(c, o_mine, o_got).reshape(64, width)


def solution(mesh):
    fine = Mesh(mesh.devices.reshape(NY, NXH, NC, NXL, NZ), ("y", "xh", "c", "xl", "z"))
    rows = P(("y", "xh", "c", "xl", "z"), None)
    pair = P(("y", "xh", "c"), None)
    return jax.shard_map(
        shards, mesh=fine, in_specs=(rows, rows, pair, pair, P()), out_specs=rows, check_vma=False
    )
```

```python
import jax
import jax.numpy as jnp
import numpy as np
from jax import lax
from jax.sharding import Mesh, PartitionSpec as P

ITERS = 4
SCALE = 3.0
NY, NXH, NC, NXL, NZ = 4, 2, 2, 2, 8
NB = NY * NXH * NC
PLANE = ("y", "xh", "c", "xl")
SWAP = [(0, 1), (1, 0)]
UP = [(i, (i + 1) % NZ) for i in range(NZ)]
DOWN = [(i, (i - 1) % NZ) for i in range(NZ)]
after = lax.optimization_barrier


def ordered(first, mine, other):
    is0 = first == 0
    return jnp.stack([jnp.where(is0, mine, other), jnp.where(is0, other, mine)])


def exchange(row, axes, n):
    return lax.all_to_all(jnp.broadcast_to(row[None], (n,) + row.shape), axes, 0, 0)


def shards(points, centroids, pair_blocks, pair_valid, sizes):
    rows, width = points.shape
    c = lax.axis_index("c")
    xl = lax.axis_index("xl")
    z = lax.axis_index("z")
    def put(buf, part, at):
        return lax.dynamic_update_slice(buf, part[None], (at % NZ, 0, 0))

    spread_cents = jnp.broadcast_to(centroids[None], (NY * NXH,) + centroids.shape)
    allc = lax.all_to_all(spread_cents, ("y", "xh"), 0, 0)
    up1 = lax.ppermute(points, "z", UP)
    down1 = lax.ppermute(points, "z", DOWN)
    pair_blocks, points, _ = after((pair_blocks, points, up1))
    slots = pair_blocks[0]
    slots_other = lax.ppermute(slots, "c", SWAP)
    up2 = lax.ppermute(up1, "z", UP)
    down2 = lax.ppermute(down1, "z", DOWN)
    pts = jnp.broadcast_to(points[None], (NZ + 2, rows, width))
    pts = put(put(pts, up1, z - 1 + NZ), down1, z + 1)
    up3 = lax.ppermute(up2, "z", UP)
    down3 = lax.ppermute(down2, "z", DOWN)
    pts = put(put(pts, up2, z - 2 + NZ), down2, z + 2)

    allc, _ = after((allc, up2))
    sel_give = allc.at[slots_other // NC].get(mode="promise_in_bounds")
    sel_got = lax.ppermute(sel_give, "c", SWAP)
    sel_mine = allc.at[slots // NC].get(mode="promise_in_bounds")
    kept = jnp.where((slots % NC == c)[:, None, None], sel_mine, sel_got)
    kept_xl = lax.ppermute(kept, "xl", SWAP)
    up3, down3, _ = after((up3, down3, kept))
    far = lax.ppermute(up3, "z", UP)
    pts = put(put(pts, up3, z - 3 + NZ), down3, z + 3)
    cents = jnp.swapaxes(ordered(xl, kept, kept_xl), 0, 1).reshape(256, width)

    valid = pair_valid[0].astype(jnp.float32)

    def kernel_of(part):
        dots = lax.dot_general(
            cents, part, (((1,), (1,)), ((), ())), preferred_element_type=jnp.float32
        )
        return (jnp.exp(SCALE * dots).reshape(2, 128, -1) * valid[:, None, None]).reshape(256, -1)

    kt = kernel_of(pts[:NZ].reshape(NZ * rows, width))
    kt = lax.dynamic_update_slice(kt, kernel_of(far), (0, ((z + 4) % NZ) * rows))
    pts = put(pts, far, z + 4)

    def totals_of(match, got):
        return jnp.sum(match[..., None] * got[:, :256].reshape(1, -1, 2, 128), axis=(1, 2))

    rowpart = jnp.sum(kt, axis=0)
    rowpart, sizes, slots, slots_other = after((rowpart, sizes, slots, slots_other))
    got = exchange(rowpart, "z", NZ)
    ids = jnp.pad(slots.astype(jnp.float32), (0, 126))
    per_row = NB * 8
    pick = (8 * slots[:, None] + 4 * jnp.arange(2, dtype=jnp.int32)[None, :] + z // 2).reshape(4)
    own = sizes.reshape(per_row, 128).at[pick].get(mode="promise_in_bounds")
    own = lax.dynamic_slice(own, (0, (z % 2) * 64), (4, 64)).reshape(2, 128)
    factor = jnp.float32(rows * 256) / jnp.sum(sizes.astype(jnp.float32))
    target_pair = own.astype(jnp.float32) * factor
    grid = lax.broadcasted_iota(jnp.int32, (4, NY * NXH), 1) * NC + c
    hits = jnp.concatenate([slots, slots_other])[:, None] == grid
    hits = [hits[i] for i in range(4)]
    got, ids, target_pair, hits, slots, pts = after((got, ids, target_pair, hits, slots, pts))
    pts = pts[:NZ].reshape(NZ * rows, width)

    for step in range(ITERS):
        if step > 0:
            got = exchange(jnp.sum(kt * scale_v[:, None], axis=0), "z", NZ)
        scale_u = 1.0 / jnp.sum(got, axis=0)
        if step < ITERS - 1:
            colpart = jnp.sum(kt * scale_u[None, :], axis=1)
            if step == 0:
                got = exchange(jnp.concatenate([colpart, ids]), PLANE, NB * NXL)
                got_ids = got[:, 256:258].astype(jnp.int32)
                match = (got_ids[None] == slots[:, None, None]).astype(jnp.float32)
                got, match = after((got, match))
            else:
                got = exchange(colpart, PLANE, NB * NXL)
            scale_v = (target_pair / totals_of(match, got)).reshape(256)
    weights = (scale_u[None, :] * kt * scale_v[:, None]).astype(jnp.bfloat16)

    def halved(part, at, axis_name):
        mine = lax.dynamic_index_in_dim(part, at, 0, keepdims=False)
        give = lax.dynamic_index_in_dim(part, 1 - at, 0, keepdims=False)
        return mine, lax.ppermute(give, axis_name, SWAP)

    ones = jnp.ones((NZ * rows, 128), jnp.bfloat16)
    tots = lax.dot_general(weights, ones, (((1,), (0,)), ((), ())), preferred_element_type=jnp.float32)
    tots = tots.reshape(2, 2, 64, 128)
    tots = jnp.swapaxes(tots, 0, 1)
    t_mine, t_got = halved(tots, xl, "xl")
    tots = t_mine + t_got
    tots = (tots, lax.ppermute(tots, "c", SWAP))

    def in_thirds(value, first):
        at = np.eye(128, dtype=np.float32)[first : first + 3]
        high = lax.reduce_precision(value, 8, 7)
        rest = value - high
        middle = lax.reduce_precision(rest, 8, 7)
        low = rest - middle
        return (high * at[:1] + middle * at[1:2] + low * at[2:]).astype(jnp.bfloat16)

    parts = []
    for k in (0, 1):
        sums = lax.dot_general(
            weights[128 * k : 128 * (k + 1)], pts, (((1,), (0,)), ((), ())), preferred_element_type=jnp.float32
        ).reshape(2, 64, width)
        mine = lax.dynamic_index_in_dim(sums, xl, 0, keepdims=False)
        give = lax.dynamic_index_in_dim(sums, 1 - xl, 0, keepdims=False).astype(jnp.bfloat16)
        got = lax.ppermute(give, "xl", SWAP)
        sums = (mine + got.astype(jnp.float32)).astype(jnp.bfloat16)
        pair = (sums, lax.ppermute(sums, "c", SWAP))
        parts.append([jnp.concatenate([pair[i], in_thirds(tots[i][k], 4 * i)], axis=1) for i in (0, 1)])
    zero = jnp.zeros((), jnp.bfloat16)

    def placed(first, second, a, b):
        return jnp.where(first[:, None, None], a, jnp.where(second[:, None, None], b, zero))

    spread = placed(hits[0], hits[1], parts[0][0], parts[1][0]) + placed(hits[2], hits[3], parts[0][1], parts[1][1])
    landed = lax.all_to_all(spread, ("y", "xh"), 0, 0)
    owned = jnp.sum(landed.astype(jnp.float32), axis=0)
    return owned[:, :width] / jnp.sum(owned[:, width:], axis=1, keepdims=True)


def solution(mesh):
    fine = Mesh(mesh.devices.reshape(NY, NXH, NC, NXL, NZ), ("y", "xh", "c", "xl", "z"))
    rows = P(("y", "xh", "c", "xl", "z"), None)
    pair = P(("y", "xh", "c"), None)
    return jax.shard_map(
        shards, mesh=fine, in_specs=(rows, rows, pair, pair, P()), out_specs=rows, check_vma=False
    )
```

```python
import jax
import jax.numpy as jnp
import numpy as np
from jax import lax
from jax.sharding import Mesh, PartitionSpec as P

ITERS = 4
SCALE = 3.0
NY, NXH, NC, NXL, NZ = 4, 2, 2, 2, 8
NB = NY * NXH * NC
PLANE = ("y", "xh", "c", "xl")
SWAP = [(0, 1), (1, 0)]
UP = [(i, (i + 1) % NZ) for i in range(NZ)]
DOWN = [(i, (i - 1) % NZ) for i in range(NZ)]
after = lax.optimization_barrier


def ordered(first, mine, other):
    is0 = first == 0
    return jnp.stack([jnp.where(is0, mine, other), jnp.where(is0, other, mine)])


def exchange(row, axes, n):
    return lax.all_to_all(jnp.broadcast_to(row[None], (n,) + row.shape), axes, 0, 0)


def shards(points, centroids, pair_blocks, pair_valid, sizes):
    rows, width = points.shape
    c = lax.axis_index("c")
    xl = lax.axis_index("xl")
    z = lax.axis_index("z")
    def put(buf, part, at):
        return lax.dynamic_update_slice(buf, part[None], (at % NZ, 0, 0))

    spread_cents = jnp.broadcast_to(centroids[None], (NY * NXH,) + centroids.shape)
    allc = lax.all_to_all(spread_cents, ("y", "xh"), 0, 0)
    up1 = lax.ppermute(points, "z", UP)
    down1 = lax.ppermute(points, "z", DOWN)
    pair_blocks, points, _ = after((pair_blocks, points, up1))
    slots = pair_blocks[0]
    slots_other = lax.ppermute(slots, "c", SWAP)
    up2 = lax.ppermute(up1, "z", UP)
    down2 = lax.ppermute(down1, "z", DOWN)
    pts = jnp.broadcast_to(points[None], (NZ + 2, rows, width))
    pts = put(put(pts, up1, z - 1 + NZ), down1, z + 1)
    up3 = lax.ppermute(up2, "z", UP)
    down3 = lax.ppermute(down2, "z", DOWN)
    pts = put(put(pts, up2, z - 2 + NZ), down2, z + 2)

    allc, _ = after((allc, up2))
    sel_give = allc.at[slots_other // NC].get(mode="promise_in_bounds")
    sel_got = lax.ppermute(sel_give, "c", SWAP)
    sel_mine = allc.at[slots // NC].get(mode="promise_in_bounds")
    kept = jnp.where((slots % NC == c)[:, None, None], sel_mine, sel_got)
    kept_xl = lax.ppermute(kept, "xl", SWAP)
    up3, down3, _ = after((up3, down3, kept))
    far = lax.ppermute(up3, "z", UP)
    pts = put(put(pts, up3, z - 3 + NZ), down3, z + 3)
    cents = jnp.swapaxes(ordered(xl, kept, kept_xl), 0, 1).reshape(256, width)

    valid = pair_valid[0].astype(jnp.float32)

    def kernel_of(part):
        dots = lax.dot_general(
            cents, part, (((1,), (1,)), ((), ())), preferred_element_type=jnp.float32
        )
        return (jnp.exp(SCALE * dots).reshape(2, 128, -1) * valid[:, None, None]).reshape(256, -1)

    kt = kernel_of(pts[:NZ].reshape(NZ * rows, width))
    kt = lax.dynamic_update_slice(kt, kernel_of(far), (0, ((z + 4) % NZ) * rows))
    pts = put(pts, far, z + 4)

    def totals_of(match, got):
        return jnp.sum(match[..., None] * got[:, :256].reshape(1, -1, 2, 128), axis=(1, 2))

    rowpart = jnp.sum(kt, axis=0)
    rowpart, sizes, slots, slots_other = after((rowpart, sizes, slots, slots_other))
    got = exchange(rowpart, "z", NZ)
    ids = jnp.pad(slots.astype(jnp.float32), (0, 126))
    per_row = NB * 8
    pick = (8 * slots[:, None] + 4 * jnp.arange(2, dtype=jnp.int32)[None, :] + z // 2).reshape(4)
    own = sizes.reshape(per_row, 128).at[pick].get(mode="promise_in_bounds")
    own = lax.dynamic_slice(own, (0, (z % 2) * 64), (4, 64)).reshape(2, 128)
    factor = jnp.float32(rows * 256) / jnp.sum(sizes.astype(jnp.float32))
    target_pair = own.astype(jnp.float32) * factor
    grid = lax.broadcasted_iota(jnp.int32, (4, NY * NXH), 1) * NC + c
    hits = jnp.concatenate([slots, slots_other])[:, None] == grid
    hits = [hits[i] for i in range(4)]
    got, ids, target_pair, hits, slots, pts = after((got, ids, target_pair, hits, slots, pts))
    pts = pts[:NZ].reshape(NZ * rows, width)

    for step in range(ITERS):
        if step > 0:
            got = exchange(jnp.sum(kt * scale_v[:, None], axis=0), "z", NZ)
        scale_u = 1.0 / jnp.sum(got, axis=0)
        if step < ITERS - 1:
            colpart = jnp.sum(kt * scale_u[None, :], axis=1)
            if step == 0:
                got = exchange(jnp.concatenate([colpart, ids]), PLANE, NB * NXL)
                got_ids = got[:, 256:258].astype(jnp.int32)
                match = (got_ids[None] == slots[:, None, None]).astype(jnp.float32)
                got, match = after((got, match))
            else:
                got = exchange(colpart, PLANE, NB * NXL)
            scale_v = (target_pair / totals_of(match, got)).reshape(256)
    weights = (scale_u[None, :] * kt * scale_v[:, None]).astype(jnp.bfloat16)

    def halved(part, at, axis_name):
        mine = lax.dynamic_index_in_dim(part, at, 0, keepdims=False)
        give = lax.dynamic_index_in_dim(part, 1 - at, 0, keepdims=False)
        return mine, lax.ppermute(give, axis_name, SWAP)

    ones = jnp.ones((NZ * rows, 128), jnp.bfloat16)
    tots = lax.dot_general(weights, ones, (((1,), (0,)), ((), ())), preferred_element_type=jnp.float32)
    tots = tots.reshape(2, 2, 64, 128)
    tots = jnp.swapaxes(tots, 0, 1)
    t_mine, t_got = halved(tots, xl, "xl")
    tots = t_mine + t_got
    tots = (tots, lax.ppermute(tots, "c", SWAP))

    def in_thirds(value, first):
        at = np.eye(128, dtype=np.float32)[first : first + 3]
        high = lax.reduce_precision(value, 8, 7)
        rest = value - high
        middle = lax.reduce_precision(rest, 8, 7)
        low = rest - middle
        return (high * at[:1] + middle * at[1:2] + low * at[2:]).astype(jnp.bfloat16)

    sides = []
    for lo, hi in ((0, width // 2), (width // 2, width)):
        sums = lax.dot_general(
            weights, pts[:, lo:hi], (((1,), (0,)), ((), ())), preferred_element_type=jnp.float32
        ).reshape(2, 2, 64, hi - lo)
        mine = lax.dynamic_index_in_dim(sums, xl, 1, keepdims=False)
        give = lax.dynamic_index_in_dim(sums, 1 - xl, 1, keepdims=False).astype(jnp.bfloat16)
        got = lax.ppermute(give, "xl", SWAP)
        sums = (mine + got.astype(jnp.float32)).astype(jnp.bfloat16)
        sides.append((sums, lax.ppermute(sums, "c", SWAP)))
    parts = [
        [
            jnp.concatenate([sides[0][i][k], sides[1][i][k], in_thirds(tots[i][k], 4 * i)], axis=1)
            for i in (0, 1)
        ]
        for k in (0, 1)
    ]
    zero = jnp.zeros((), jnp.bfloat16)

    def placed(first, second, a, b):
        return jnp.where(first[:, None, None], a, jnp.where(second[:, None, None], b, zero))

    spread = placed(hits[0], hits[1], parts[0][0], parts[1][0]) + placed(hits[2], hits[3], parts[0][1], parts[1][1])
    landed = lax.all_to_all(spread, ("y", "xh"), 0, 0)
    owned = jnp.sum(landed.astype(jnp.float32), axis=0)
    return owned[:, :width] / jnp.sum(owned[:, width:], axis=1, keepdims=True)


def solution(mesh):
    fine = Mesh(mesh.devices.reshape(NY, NXH, NC, NXL, NZ), ("y", "xh", "c", "xl", "z"))
    rows = P(("y", "xh", "c", "xl", "z"), None)
    pair = P(("y", "xh", "c"), None)
    return jax.shard_map(
        shards, mesh=fine, in_specs=(rows, rows, pair, pair, P()), out_specs=rows, check_vma=False
    )
```

```python
import jax
import jax.numpy as jnp
import numpy as np
from jax import lax
from jax.sharding import Mesh, PartitionSpec as P

ITERS = 4
SCALE = 3.0
NY, NXH, NC, NXL, NZ = 4, 2, 2, 2, 8
NB = NY * NXH * NC
PLANE = ("y", "xh", "c", "xl")
SWAP = [(0, 1), (1, 0)]
UP = [(i, (i + 1) % NZ) for i in range(NZ)]
DOWN = [(i, (i - 1) % NZ) for i in range(NZ)]
after = lax.optimization_barrier


def ordered(first, mine, other):
    is0 = first == 0
    return jnp.stack([jnp.where(is0, mine, other), jnp.where(is0, other, mine)])


def exchange(row, axes, n):
    return lax.all_to_all(jnp.broadcast_to(row[None], (n,) + row.shape), axes, 0, 0)


def shards(points, centroids, pair_blocks, pair_valid, sizes):
    rows, width = points.shape
    c = lax.axis_index("c")
    xl = lax.axis_index("xl")
    z = lax.axis_index("z")
    def put(buf, part, at):
        return lax.dynamic_update_slice(buf, part[None], (at % NZ, 0, 0))

    spread_cents = jnp.broadcast_to(centroids[None], (NY * NXH,) + centroids.shape)
    allc = lax.all_to_all(spread_cents, ("y", "xh"), 0, 0)
    up1 = lax.ppermute(points, "z", UP)
    down1 = lax.ppermute(points, "z", DOWN)
    pair_blocks, points, _ = after((pair_blocks, points, up1))
    slots = pair_blocks[0]
    slots_other = lax.ppermute(slots, "c", SWAP)
    up2 = lax.ppermute(up1, "z", UP)
    down2 = lax.ppermute(down1, "z", DOWN)
    pts = jnp.broadcast_to(points[None], (NZ + 2, rows, width))
    pts = put(put(pts, up1, z - 1 + NZ), down1, z + 1)
    up3 = lax.ppermute(up2, "z", UP)
    down3 = lax.ppermute(down2, "z", DOWN)
    pts = put(put(pts, up2, z - 2 + NZ), down2, z + 2)

    allc, _ = after((allc, up2))
    sel_give = allc.at[slots_other // NC].get(mode="promise_in_bounds")
    sel_got = lax.ppermute(sel_give, "c", SWAP)
    sel_mine = allc.at[slots // NC].get(mode="promise_in_bounds")
    kept = jnp.where((slots % NC == c)[:, None, None], sel_mine, sel_got)
    kept_xl = lax.ppermute(kept, "xl", SWAP)
    up3, down3, _ = after((up3, down3, kept))
    far = lax.ppermute(up3, "z", UP)
    pts = put(put(pts, up3, z - 3 + NZ), down3, z + 3)
    cents = jnp.swapaxes(ordered(xl, kept, kept_xl), 0, 1).reshape(256, width)

    valid = pair_valid[0].astype(jnp.float32)

    def kernel_of(part):
        dots = lax.dot_general(
            cents, part, (((1,), (1,)), ((), ())), preferred_element_type=jnp.float32
        )
        return (jnp.exp(SCALE * dots).reshape(2, 128, -1) * valid[:, None, None]).reshape(256, -1)

    kt = kernel_of(pts[:NZ].reshape(NZ * rows, width))
    kt = lax.dynamic_update_slice(kt, kernel_of(far), (0, ((z + 4) % NZ) * rows))

    def totals_of(match, got):
        return jnp.sum(match[..., None] * got[:, :256].reshape(1, -1, 2, 128), axis=(1, 2))

    sizes, slots, slots_other, _ = after((sizes, slots, slots_other, kept))
    ids = jnp.pad(slots.astype(jnp.float32), (0, 126))
    per_row = NB * 8
    pick = (8 * slots[:, None] + 4 * jnp.arange(2, dtype=jnp.int32)[None, :] + z // 2).reshape(4)
    own = sizes.reshape(per_row, 128).at[pick].get(mode="promise_in_bounds")
    own = lax.dynamic_slice(own, (0, (z % 2) * 64), (4, 64)).reshape(2, 128)
    factor = jnp.float32(rows * 256) / jnp.sum(sizes.astype(jnp.float32))
    target_pair = own.astype(jnp.float32) * factor
    grid = lax.broadcasted_iota(jnp.int32, (4, NY * NXH), 1) * NC + c
    hits = jnp.concatenate([slots, slots_other])[:, None] == grid
    hits = [hits[i] for i in range(4)]
    kt, ids, target_pair, hits, slots = after((kt, ids, target_pair, hits, slots))

    scale_v = jnp.ones((256,), jnp.float32)
    for step in range(ITERS):
        rowpart = jnp.sum(kt if step == 0 else kt * scale_v[:, None], axis=0)
        if step == ITERS - 1:
            rowpart, pts, far = after((rowpart, pts, far))
        got = exchange(rowpart, "z", NZ)
        if step == ITERS - 1:
            pts = put(pts, far, z + 4)[:NZ].reshape(NZ * rows, width)
            got, pts = after((got, pts))
        scale_u = 1.0 / jnp.sum(got, axis=0)
        if step < ITERS - 1:
            colpart = jnp.sum(kt * scale_u[None, :], axis=1)
            if step == 0:
                got = exchange(jnp.concatenate([colpart, ids]), PLANE, NB * NXL)
                got_ids = got[:, 256:258].astype(jnp.int32)
                match = (got_ids[None] == slots[:, None, None]).astype(jnp.float32)
                got, match = after((got, match))
            else:
                got = exchange(colpart, PLANE, NB * NXL)
            scale_v = (target_pair / totals_of(match, got)).reshape(256)
    weights = (scale_u[None, :] * kt * scale_v[:, None]).astype(jnp.bfloat16)

    def halved(part, at, axis_name):
        mine = lax.dynamic_index_in_dim(part, at, 0, keepdims=False)
        give = lax.dynamic_index_in_dim(part, 1 - at, 0, keepdims=False)
        return mine, lax.ppermute(give, axis_name, SWAP)

    ones = jnp.ones((NZ * rows, 128), jnp.bfloat16)
    tots = lax.dot_general(weights, ones, (((1,), (0,)), ((), ())), preferred_element_type=jnp.float32)
    tots = tots.reshape(2, 2, 64, 128)
    tots = jnp.swapaxes(tots, 0, 1)
    t_mine, t_got = halved(tots, xl, "xl")
    tots = t_mine + t_got
    tots = (tots, lax.ppermute(tots, "c", SWAP))

    def in_thirds(value, first):
        at = np.eye(128, dtype=np.float32)[first : first + 3]
        high = lax.reduce_precision(value, 8, 7)
        rest = value - high
        middle = lax.reduce_precision(rest, 8, 7)
        low = rest - middle
        return (high * at[:1] + middle * at[1:2] + low * at[2:]).astype(jnp.bfloat16)

    parts = []
    for k in (0, 1):
        part = weights[128 * k : 128 * (k + 1)]
        if k == 1:
            part, _ = after((part, give))
        sums = lax.dot_general(
            part, pts, (((1,), (0,)), ((), ())), preferred_element_type=jnp.float32
        ).reshape(2, 64, width)
        mine = lax.dynamic_index_in_dim(sums, xl, 0, keepdims=False)
        give = lax.dynamic_index_in_dim(sums, 1 - xl, 0, keepdims=False).astype(jnp.bfloat16)
        got = lax.ppermute(give, "xl", SWAP)
        sums = (mine + got.astype(jnp.float32)).astype(jnp.bfloat16)
        pair = (sums, lax.ppermute(sums, "c", SWAP))
        parts.append([jnp.concatenate([pair[i], in_thirds(tots[i][k], 4 * i)], axis=1) for i in (0, 1)])
    zero = jnp.zeros((), jnp.bfloat16)

    def placed(first, second, a, b):
        return jnp.where(first[:, None, None], a, jnp.where(second[:, None, None], b, zero))

    spread = placed(hits[0], hits[1], parts[0][0], parts[1][0]) + placed(hits[2], hits[3], parts[0][1], parts[1][1])
    landed = lax.all_to_all(spread, ("y", "xh"), 0, 0)
    owned = jnp.sum(landed.astype(jnp.float32), axis=0)
    return owned[:, :width] / jnp.sum(owned[:, width:], axis=1, keepdims=True)


def solution(mesh):
    fine = Mesh(mesh.devices.reshape(NY, NXH, NC, NXL, NZ), ("y", "xh", "c", "xl", "z"))
    rows = P(("y", "xh", "c", "xl", "z"), None)
    pair = P(("y", "xh", "c"), None)
    return jax.shard_map(
        shards, mesh=fine, in_specs=(rows, rows, pair, pair, P()), out_specs=rows, check_vma=False
    )
```
